512 devices in a mesh: row: 16 (over x, y_lo, core), col: 32 (over y_hi, z).
Axes of the slice: x: 4, y: 4 (y_hi: 2, y_lo: 2; y = y_hi * 2 + y_lo), z: 16, core: 2. Of those that a mesh axis runs over, the one named last changes fastest.
Arguments:
- basis_new_left: float32 [3072, 3072], P('row', 'col'), may hold values from -0.109375 to 0.109375
- basis_old_left: float32 [3072, 3072], P('row', 'col'), may hold values from -0.109375 to 0.109375
- basis_new_right: float32 [3072, 3072], P('row', 'col'), may hold values from -0.109375 to 0.109375
- basis_old_right: float32 [3072, 3072], P('row', 'col'), may hold values from -0.109375 to 0.109375
- moment: float32 [3072, 3072], P('row', 'col'), may hold values from -6 to 6
Outputs:
- rebased: float32 [3072, 3072], P('row', 'col')
The draws below stay inside these ranges and needn't reach their ends.
All inputs are finite; a program needn't handle non-finite values.
Results may differ from the reference program's by a relative error of at most 0.000094.
Values sent between devices are 32-bit elements; how exact they have to be, the bound alone decides.
A program may use at most 64 MiB of HBM per device.

```python
import jax
import jax.numpy as jnp
from jax import lax

N = 3072


def level_of(stream_key, dims, cuts, least, largest):
    factor_of, own = 1.0, jax.random.fold_in(stream_key, 6)
    for position, shards_of in cuts:
        heights = jnp.exp(jax.random.uniform(jax.random.fold_in(own, position), (shards_of,), jnp.float32, least / len(cuts), largest / len(cuts)))
        factor_of = factor_of * jnp.repeat(heights, dims[position] // shards_of).reshape([-1 if axis == position else 1 for axis in range(len(dims))])
    return factor_of


def centred(own_key, dims, deviation, bound, split=(), held_as=jnp.bfloat16):
    entries = deviation * jax.random.normal(own_key, dims, jnp.float32)
    if split:
        entries = entries * level_of(own_key, dims, split, -0.22, 0.18)
    return jnp.clip(entries, -bound, bound).astype(held_as)


def setup_inputs(seed: int = 0) -> dict:
    streams_of = jax.random.split(jax.random.key(seed), 6)
    return {
        "basis_new_left": centred(streams_of[0], (N, N), N ** -0.5, 0.109375, ((0, 16), (1, 32)), jnp.float32),
        "basis_old_left": centred(streams_of[1], (N, N), N ** -0.5, 0.109375, ((0, 16), (1, 32)), jnp.float32),
        "basis_new_right": centred(streams_of[2], (N, N), N ** -0.5, 0.109375, ((0, 16), (1, 32)), jnp.float32),
        "basis_old_right": centred(streams_of[3], (N, N), N ** -0.5, 0.109375, ((0, 16), (1, 32)), jnp.float32),
        "moment": centred(streams_of[4], (N, N), 1.0, 6.0, ((0, 16), (1, 32)), jnp.float32),
    }


def reference(basis_new_left, basis_old_left, basis_new_right, basis_old_right, moment):
    highest = lax.Precision.HIGHEST
    right = jnp.dot(basis_old_right.T, basis_new_right, precision=highest, preferred_element_type=jnp.float32)
    left = jnp.dot(basis_new_left.T, basis_old_left, precision=highest, preferred_element_type=jnp.float32)
    rotated = jnp.dot(moment, right, precision=highest, preferred_element_type=jnp.float32)
    return jnp.dot(left, rotated, precision=highest, preferred_element_type=jnp.float32)
```

```python
import functools

import jax
import jax.numpy as jnp
from jax import lax
from jax.experimental import pallas as pl
from jax.experimental.pallas import tpu as pltpu
from jax.sharding import PartitionSpec as P

MESH = pl.DeviceIdType.MESH
F32, BF16 = jnp.float32, jnp.bfloat16
OLD_R, MOM, OLD_L, NEW_L = 0, 1, 2, 3
NCH = 2
OFFSETS = (0.0, 0.2, 6.0, 6.2)
NN = (((1,), (0,)), ((), ()))
NT = (((1,), (1,)), ((), ()))


def split(value):
    high = value.astype(BF16)
    return high, (value - high.astype(F32)).astype(BF16)


def dot3(a, b, dims):
    def one(u, v):
        return lax.dot_general(u, v, dims, preferred_element_type=F32)

    return one(a[0], b[0]) + (one(a[0], b[1]) + one(a[1], b[0]))


def kernel(c_ref, m_ref, b_ref, a_ref, d_ref, o_ref, *scratch):
    (pk, rb, dsend, drecv, dth, dtl, tmp, rp, rsib, rsum, rrs, rg, mh, ml, bh, bl, ah, al,
     tp, trecv, tfin, tg, th, tl, up, urecv, vp, vsib, vsum, vrecv,
     ring_s, ring_r, d_s, d_r, g2_s, g2_r, g3_s, g3_r, g5_s, g5_r, g6_s, g6_r,
     te_s, te_r, tm_s, tm_r, tf_s, tf_r, ue_s, ue_r, vs_s, vs_r, vr_s, vr_r) = scratch
    r, q = lax.axis_index("row"), lax.axis_index("col")
    p, c = r // 2, lax.rem(r, 2)
    h, z = q // 16, lax.rem(q, 16)
    sibling = (p * 2 + (1 - c), q)
    partner = (r, (1 - h) * 16 + z)
    ring_to = ((r, h * 16 + lax.rem(z + 1, 16)), (r, h * 16 + lax.rem(z + 15, 16)))

    def chip(k, plane):
        return (lax.rem(p + k, 8) * 2 + c, plane * 16 + z)

    barrier = pltpu.get_barrier_semaphore()
    greeted = [sibling, ring_to[0], ring_to[1], partner]
    greeted += [chip(k, plane) for k in range(1, 8) for plane in (h, 1 - h)]
    for device in greeted:
        pl.semaphore_signal(barrier, inc=1, device_id=device, device_id_type=MESH)

    own = (c_ref, m_ref, b_ref, a_ref)
    for index, ref in enumerate(own):
        pk[index, :, 0:96] = ref[0:144, :]
        for part in range(3):
            pk[index, 48 * part:48 * part + 48, 96:128] = ref[144:192, 32 * part:32 * part + 32]
    dsend[:, 0:96] = d_ref[...]
    dsend[:, 96:128] = jnp.zeros((192, 32), F32)
    pl.semaphore_wait(barrier, len(greeted))

    def remote(src, dst, send, recv, device):
        return pltpu.make_async_remote_copy(
            src_ref=src, dst_ref=dst, send_sem=send, recv_sem=recv, device_id=device, device_id_type=MESH
        )

    finish = []

    def go(copy):
        copy.start()
        finish.append(copy)
        return copy

    def ring(m, d, s, ch):
        if s == 8:
            rows, dst = pl.ds(72 * d, 72), rb.at[m, 0, 7]
        else:
            rows, dst = pl.ds(ch * (144 // NCH), 144 // NCH), rb.at[m, d, s - 1]
        src = pk.at[m] if s == 1 else rb.at[m, d, s - 2]
        return remote(src.at[rows], dst.at[rows], ring_s.at[m, d, s - 1, ch], ring_r.at[m, d, s - 1, ch], ring_to[d])

    waited = set()

    def arrived(m, d, s, ch):
        if s >= 1 and (m, d, s, ch) not in waited:
            waited.add((m, d, s, ch))
            ring(m, d, s, ch).wait_recv()

    def send_step(m, s):
        for ch in range(NCH if s < 8 else 1):
            for d in range(2):
                for before in ([ch] if s < 8 else range(NCH)):
                    arrived(m, d, s - 1, before)
                go(ring(m, d, s, ch))

    def unpacked(src):
        lane = lax.broadcasted_iota(jnp.int32, (144, 128), 1)
        tmp[0:144, :] = jnp.where(lane < 96, src[...], 0.0)
        for part in range(3):
            tmp[144:192, 32 * part:32 * part + 32] = src[48 * part:48 * part + 48, 96:128]
        return split(tmp[...])

    def store(m, d, e, value):
        high, low = value
        if m == OLD_R:
            lanes = slice(128 * (e % 4), 128 * (e % 4) + 128)
            rp[d, e // 4, :, lanes] = dot3((dth[...], dtl[...]), value, NN)
        elif m == MOM:
            mh[d, :, 128 * e:128 * e + 128] = high
            ml[d, :, 128 * e:128 * e + 128] = low
        else:
            origin = lax.rem(z + (16 - (e + 1) if d == 0 else e), 16)
            lanes = pl.ds(pl.multiple_of(origin * 128, 128), 128)
            hs, ls = (bh, bl) if m == OLD_L else (ah, al)
            hs[:, lanes] = high
            ls[:, lanes] = low

    def own_block(m):
        tmp[:, 0:96] = own[m][...]
        store(m, 1, 0, split(tmp[...]))

    def take(m, s):
        for d in range(2):
            if s == 8:
                arrived(m, d, 8, 0)
            else:
                for ch in range(NCH):
                    arrived(m, d, s, ch)
        store(m, 0, s - 1, unpacked(rb.at[m, 0, s - 1]))
        if s < 8:
            store(m, 1, s, unpacked(rb.at[m, 1, s - 1]))

    def rows_of(index):
        return pl.ds(pl.multiple_of(index * 24, 8), 24)

    def r_sibling(g):
        go(remote(rp.at[1 - c, g], rsib.at[g], g2_s.at[g], g2_r.at[g], sibling))

    def r_scatter(g):
        remote(rp.at[1 - c, g], rsib.at[g], g2_s.at[g], g2_r.at[g], sibling).wait_recv()
        rsum[g] = rp[c, g] + rsib[g]
        for k in range(1, 8):
            go(r_piece(g, k))

    def r_piece(g, k):
        target = lax.rem(p + k, 8)
        return remote(rsum.at[g, rows_of(target)], rrs.at[g, k - 1], g3_s.at[g, k - 1], g3_r.at[g, k - 1], chip(k, h))

    def r_whole(g, k):
        mine = rg.at[c, g, rows_of(p)]
        return remote(mine, mine, g5_s.at[g, k - 1], g5_r.at[g, k - 1], chip(k, h))

    def r_gather(g):
        total = rsum[g, rows_of(p), :]
        for k in range(1, 8):
            r_piece(g, k).wait_recv()
            total = total + rrs[g, k - 1]
        rg[c, g, rows_of(p), :] = total
        for k in range(1, 8):
            go(r_whole(g, k))

    def r_forward(g):
        for k in range(1, 8):
            r_whole(g, k).wait_recv()
        go(remote(rg.at[c, g], rg.at[c, g], g6_s.at[g], g6_r.at[g], sibling))

    def t_partial():
        for g in range(2):
            remote(rg.at[c, g], rg.at[c, g], g6_s.at[g], g6_r.at[g], sibling).wait_recv()
        for half in range(2):
            total = None
            for d in range(2):
                for g in range(2):
                    lanes = slice(512 * g, 512 * g + 512)
                    rows = slice(96 * half, 96 * half + 96)
                    term = dot3(split(rg[d, g]), (mh[d, rows, lanes], ml[d, rows, lanes]), NT)
                    total = term if total is None else total + term
            tp[:, 128 * half:128 * half + 96] = total
            tp[:, 128 * half + 96:128 * half + 128] = jnp.zeros((192, 32), F32)
        go(t_exchange())

    def half_of(plane):
        return pl.ds(pl.multiple_of(plane * 96, 8), 96)

    def t_exchange():
        return remote(tp.at[half_of(1 - h)], trecv, te_s.at[0], te_r.at[0], partner)

    plane_of = r // 8

    def t_piece(k):
        return remote(tfin, tg.at[c, lax.rem(p, 4), h], tm_s.at[k], tm_r.at[lax.rem(p, 4), h], chip(k, plane_of))

    def t_spread():
        t_exchange().wait_recv()
        tfin[...] = tp[half_of(h), :] + trecv[...]
        for k in range(1, 8):
            go(t_piece(k))

        @pl.when(plane_of != h)
        def _():
            t_piece(0).start()

        @pl.when(plane_of == h)
        def _():
            pltpu.make_async_copy(tfin, tg.at[c, lax.rem(p, 4), h], tm_r.at[lax.rem(p, 4), h]).start()

    def t_forward():
        for j in range(4):
            for plane in range(2):
                pltpu.make_async_copy(tfin, tg.at[c, j, plane], tm_r.at[j, plane]).wait()
        go(remote(tg.at[c], tg.at[c], tf_s.at[0], tf_r.at[0], sibling))

    def u_partial():
        remote(tg.at[c], tg.at[c], tf_s.at[0], tf_r.at[0], sibling).wait_recv()
        for core in range(2):
            for j in range(4):
                for plane in range(2):
                    high, low = split(tg[core, j, plane])
                    lanes = slice(256 * (2 * j + core), 256 * (2 * j + core) + 256)
                    th[96 * plane:96 * plane + 96, lanes] = high
                    tl[96 * plane:96 * plane + 96, lanes] = low
        up[:, 0:192] = dot3((th[...], tl[...]), (bh[...], bl[...]), NT)
        up[:, 192:256] = jnp.zeros((192, 64), F32)
        go(remote(up, urecv, ue_s.at[0], ue_r.at[0], partner))

    def v_sibling(k):
        return remote(vp.at[1 - c, k], vsib.at[k], vs_s.at[k], vs_r.at[k], sibling)

    def v_partial():
        remote(up, urecv, ue_s.at[0], ue_r.at[0], partner).wait_recv()
        whole = split(up[:, 0:192] + urecv[:, 0:192])
        for k in range(4):
            for core in range(2):
                lanes = slice(256 * (2 * k + core), 256 * (2 * k + core) + 256)
                vp[core, k] = dot3(whole, (ah[:, lanes], al[:, lanes]), NN)
            go(v_sibling(k))

    def v_piece(k, plane):
        target = lax.rem(p + k, 4)
        return remote(
            vsum.at[target, pl.ds(96 * plane, 96)], vrecv.at[p], vr_s.at[k, plane], vr_r.at[p],
            ((4 * h + target) * 2 + c, plane * 16 + z),
        )

    def v_scatter():
        for k in range(4):
            v_sibling(k).wait_recv()
            vsum[k] = vp[c, k] + vsib[k]
        for k in range(4):
            for plane in range(2):
                target = lax.rem(p + k, 4)
                here = jnp.logical_and(4 * h + target == p, h == plane)

                @pl.when(jnp.logical_not(here))
                def _():
                    v_piece(k, plane).start()

                @pl.when(here)
                def _():
                    pltpu.make_async_copy(vsum.at[target, pl.ds(96 * plane, 96)], vrecv.at[p], vr_r.at[p]).start()

    def v_result():
        total = None
        for k in range(8):
            pltpu.make_async_copy(vsum.at[0, pl.ds(0, 96)], vrecv.at[k], vr_r.at[k]).wait()
            total = vrecv[k] if total is None else total + vrecv[k]
        turned = total.T
        o_ref[0:96, :] = turned[0:96, :]
        o_ref[96:192, :] = turned[128:224, :]

    events = sorted((OFFSETS[m] + s, m, s) for m in range(4) for s in range(1, 10))
    hooks = {
        (OLD_R, 6): [lambda: r_sibling(0)],
        (OLD_R, 7): [lambda: r_scatter(0)],
        (OLD_R, 9): [lambda: r_sibling(1)],
        (MOM, 9): [lambda: r_gather(0)],
        (OLD_L, 3): [lambda: r_scatter(1)],
        (OLD_L, 4): [lambda: r_gather(1)],
        (NEW_L, 4): [lambda: r_forward(0)],
        (OLD_L, 5): [lambda: r_forward(1)],
        (NEW_L, 5): [t_partial],
        (NEW_L, 6): [t_spread],
        (NEW_L, 7): [t_forward],
        (OLD_L, 9): [u_partial],
        (NEW_L, 9): [v_partial, v_scatter, v_result],
    }
    tmp[:, 96:128] = jnp.zeros((192, 32), F32)
    d_copy = remote(dsend, drecv, d_s.at[0], d_r.at[0], partner)
    for _, m, s in events:
        if s <= 8:
            send_step(m, s)
        if s == 1:
            if m == OLD_R:
                go(d_copy)
        if s == 2 and m == OLD_R:
            d_copy.wait_recv()
            for ref, plane in ((dsend, h), (drecv, 1 - h)):
                high, low = split(ref[...].T[0:96, :])
                dth[pl.ds(pl.multiple_of(plane * 96, 16), 96), :] = high
                dtl[pl.ds(pl.multiple_of(plane * 96, 16), 96), :] = low
            own_block(OLD_R)
        elif s == 1 and m != OLD_R:
            own_block(m)
        if s >= 2:
            take(m, s - 1)
        for hook in hooks.get((m, s), []):
            hook()

    for copy in finish:
        copy.wait_send()

    @pl.when(plane_of != h)
    def _():
        t_piece(0).wait_send()

    for k in range(4):
        for plane in range(2):
            here = jnp.logical_and(4 * h + lax.rem(p + k, 4) == p, h == plane)

            @pl.when(jnp.logical_not(here))
            def _():
                v_piece(k, plane).wait_send()


def local(basis_new_left, basis_old_left, basis_new_right, basis_old_right, moment):
    vmem, dma = pltpu.VMEM, pltpu.SemaphoreType.DMA
    scratch = [
        vmem((4, 144, 128), F32), vmem((4, 2, 8, 144, 128), F32),
        vmem((192, 128), F32), vmem((192, 128), F32), vmem((192, 192), BF16), vmem((192, 192), BF16),
        vmem((192, 128), F32),
        vmem((2, 2, 192, 512), F32), vmem((2, 192, 512), F32), vmem((2, 192, 512), F32),
        vmem((2, 7, 24, 512), F32), vmem((2, 2, 192, 512), F32),
        vmem((2, 192, 1024), BF16), vmem((2, 192, 1024), BF16),
        vmem((192, 2048), BF16), vmem((192, 2048), BF16), vmem((192, 2048), BF16), vmem((192, 2048), BF16),
        vmem((192, 256), F32), vmem((96, 256), F32), vmem((96, 256), F32), vmem((2, 4, 2, 96, 256), F32),
        vmem((192, 2048), BF16), vmem((192, 2048), BF16),
        vmem((192, 256), F32), vmem((192, 256), F32),
        vmem((2, 4, 192, 256), F32), vmem((4, 192, 256), F32), vmem((4, 192, 256), F32), vmem((8, 96, 256), F32),
        dma((4, 2, 8, NCH)), dma((4, 2, 8, NCH)), dma((1,)), dma((1,)),
        dma((2,)), dma((2,)), dma((2, 7)), dma((2, 7)), dma((2, 7)), dma((2, 7)), dma((2,)), dma((2,)),
        dma((1,)), dma((1,)), dma((8,)), dma((4, 2)), dma((1,)), dma((1,)), dma((1,)), dma((1,)),
        dma((4,)), dma((4,)), dma((4, 2)), dma((8,)),
    ]
    return pl.pallas_call(
        kernel,
        out_shape=jax.ShapeDtypeStruct((192, 96), F32),
        in_specs=[pl.BlockSpec(memory_space=pltpu.VMEM)] * 5,
        out_specs=pl.BlockSpec(memory_space=pltpu.VMEM),
        scratch_shapes=scratch,
        compiler_params=pltpu.CompilerParams(
            collective_id=0, has_side_effects=True, vmem_limit_bytes=48 << 20
        ),
    )(basis_old_right, moment, basis_old_left, basis_new_left, basis_new_right)


def solution(mesh):
    placed = (P("row", "col"),) * 5
    return jax.shard_map(local, mesh=mesh, in_specs=placed, out_specs=P("row", "col"), check_vma=False)
```

```python
import functools

import jax
import jax.numpy as jnp
from jax import lax
from jax.experimental import pallas as pl
from jax.experimental.pallas import tpu as pltpu
from jax.sharding import PartitionSpec as P

MESH = pl.DeviceIdType.MESH
F32, BF16 = jnp.float32, jnp.bfloat16
OLD_R, MOM, OLD_L, NEW_L = 0, 1, 2, 3
NCH = 2
STARTS = (0.0, 0.5, 13.0, 13.5)
RATES = (4.0, 3.6, 4.4, 4.4)
EVENTS = [(STARTS[0] + RATES[0] * s, "fast", OLD_R, s) for s in range(5)]
EVENTS += [(STARTS[m] + RATES[m] * (s - 1), "ring", m, s) for m in (MOM, OLD_L, NEW_L) for s in range(1, 10)]
EVENTS += [
    (0.1, "spread_d", None, 0), (0.2, "load_m", None, 0), (0.8, "swap_start", OLD_L, 0), (0.9, "swap_start", NEW_L, 0),
    (3.0, "turn_d", None, 0), (12.8, "swap_end", OLD_L, 0), (12.9, "swap_end", NEW_L, 0),
    (8.1, "r_sibling", 0, 0), (10.0, "r_scatter", 0, 0), (14.0, "r_gather", 0, 0), (18.5, "r_forward", 0, 0),
    (16.1, "r_sibling", 1, 0), (17.8, "r_scatter", 1, 0), (22.5, "r_gather", 1, 0), (27.0, "r_forward", 1, 0),
    (29.5, "t_partial", None, 0), (33.0, "t_spread", None, 0),
    (38.0, "t_forward", None, 0), (48.3, "u_partial", None, 0),
    (49.0, "v_partial", None, 0), (49.1, "v_scatter", None, 0), (49.2, "v_result", None, 0),
]
NN = (((1,), (0,)), ((), ()))
NT = (((1,), (1,)), ((), ()))


def split(value):
    high = value.astype(BF16)
    return high, (value - high.astype(F32)).astype(BF16)


def dot3(a, b, dims):
    def one(u, v):
        return lax.dot_general(u, v, dims, preferred_element_type=F32)

    return one(a[0], b[0]) + (one(a[0], b[1]) + one(a[1], b[0]))


def kernel(c_ref, m_ref, b_ref, a_ref, d_ref, o_ref, *scratch):
    (inp, sw, wide, turned, pk, rb, dsend, drecv, dth, dtl, tmp, rp, rsib, rsum, rrs, rg, mh, ml, bh, bl, ah, al,
     tp, trecv, tfin, tg, th, tl, up, urecv, vp, vsib, vsum, vrecv,
     in_s, sw_s, sw_r, ring_s, ring_r, d_s, d_r, g2_s, g2_r, g3_s, g3_r, g5_s, g5_r, g6_s, g6_r,
     te_s, te_r, tm_s, tm_r, tf_s, tf_r, ue_s, ue_r, vs_s, vs_r, vr_s, vr_r) = scratch
    r, q = lax.axis_index("row"), lax.axis_index("col")
    p, c = r // 2, lax.rem(r, 2)
    h, z = q // 16, lax.rem(q, 16)
    half, place = p // 4, lax.rem(p, 4)
    sibling = (p * 2 + (1 - c), q)
    partner = (r, (1 - h) * 16 + z)
    ring_to = tuple((r, h * 16 + lax.rem(z + k, 16)) for k in (1, 15, 2, 14))

    def chip(k):
        return (lax.rem(p + k, 8) * 2 + c, q)

    def near(k, other):
        return ((4 * half + lax.rem(place + k, 4)) * 2 + c, ((1 - h) if other else h) * 16 + z)

    across = ((4 * (1 - half) + place) * 2 + c, (1 - h) * 16 + z)

    barrier = pltpu.get_barrier_semaphore()
    greeted = [sibling, across, *ring_to]
    greeted += [chip(k) for k in range(1, 8)] + [near(k, True) for k in range(4)]
    for device in greeted:
        pl.semaphore_signal(barrier, inc=1, device_id=device, device_id_type=MESH)

    loads = [pltpu.make_async_copy(ref, inp.at[i], in_s.at[i]) for i, ref in enumerate((c_ref, d_ref, m_ref, b_ref, a_ref))]
    for load in loads:
        load.start()

    def pack(source, dst):
        dst[:, 0:96] = source[0:144, :]
        for part in range(3):
            dst[48 * part:48 * part + 48, 96:128] = source[144:192, 32 * part:32 * part + 32]

    loads[0].wait()
    pack(inp.at[0], pk.at[OLD_R])
    pl.semaphore_wait(barrier, len(greeted))

    def remote(src, dst, send, recv, device):
        return pltpu.make_async_remote_copy(
            src_ref=src, dst_ref=dst, send_sem=send, recv_sem=recv, device_id=device, device_id_type=MESH
        )

    finish = []

    def go(copy):
        copy.start()
        finish.append(copy)
        return copy

    def ring(m, d, s, ch):
        if s == 8:
            rows, dst = pl.ds(72 * d, 72), rb.at[m, 0, 7]
        else:
            rows, dst = pl.ds(ch * (144 // NCH), 144 // NCH), rb.at[m, d, s - 1]
        back = 2 if m == OLD_R and s % 2 == 0 else 1
        src = pk.at[m] if s == back else rb.at[m, d, s - back - 1]
        return remote(
            src.at[rows], dst.at[rows], ring_s.at[m, d, s - 1, ch], ring_r.at[m, d, s - 1, ch],
            ring_to[d + 2 * (back - 1)],
        )

    waited = set()

    def arrived(m, d, s, ch):
        if s >= 1 and (m, d, s, ch) not in waited:
            waited.add((m, d, s, ch))
            ring(m, d, s, ch).wait_recv()

    def send_step(m, s):
        for ch in range(NCH if s < 8 else 1):
            for d in range(2):
                for before in ([ch] if s < 8 else range(NCH)):
                    arrived(m, d, s - 1, before)
                go(ring(m, d, s, ch))

    def fast_step(s):
        for ch in range(NCH):
            if s > 0:
                for d in range(2):
                    arrived(OLD_R, d, 2 * s, ch)
            if s < 3:
                for d in range(2):
                    go(ring(OLD_R, d, 2 * s + 2, ch))
            elif ch == NCH - 1:
                for d in range(2):
                    go(ring(OLD_R, d, 8, 0))
            for d in range(2):
                go(ring(OLD_R, d, 2 * s + 1, ch))

    def unpacked(src):
        lane = lax.broadcasted_iota(jnp.int32, (144, 128), 1)
        tmp[0:144, :] = jnp.where(lane < 96, src[...], 0.0)
        for part in range(3):
            tmp[144:192, 32 * part:32 * part + 32] = src[48 * part:48 * part + 48, 96:128]
        return split(tmp[...])

    def store(m, d, e, value):
        high, low = value
        if m == OLD_R:
            rp[d, :, 96 * e:96 * e + 96] = dot3((dth[...], dtl[...]), value, NN)[:, 0:96]
        elif m == MOM:
            mh[d, :, 96 * e:96 * e + 96] = high[:, 0:96]
            ml[d, :, 96 * e:96 * e + 96] = low[:, 0:96]
        else:
            origin = lax.rem(z + (16 - (e + 1) if d == 0 else e), 16)
            lanes = pl.ds(pl.multiple_of(origin * 128, 128), 128)
            hs, ls = (bh, bl) if m == OLD_L else (ah, al)
            hs[:, lanes] = high
            ls[:, lanes] = low

    def own_block(m):
        if m == OLD_R or m == MOM:
            tmp[:, 0:96] = inp[0 if m == OLD_R else 2]
            store(m, 1, 0, split(tmp[...]))
        else:
            store(m, 1, 0, unpacked(pk.at[m]))

    def swap(m):
        return remote(sw.at[m - 2], pk.at[m], sw_s.at[m - 2], sw_r.at[m - 2], across)

    def swap_start(m):
        loads[m + 1].wait()
        pack(inp.at[m + 1], sw.at[m - 2])

        @pl.when(half != h)
        def _():
            swap(m).start()

        @pl.when(half == h)
        def _():
            pltpu.make_async_copy(sw.at[m - 2], pk.at[m], sw_r.at[m - 2]).start()

    def swap_end(m):
        pltpu.make_async_copy(sw.at[m - 2], pk.at[m], sw_r.at[m - 2]).wait()

    def take(m, s):
        for d in range(2):
            if s == 8:
                arrived(m, d, 8, 0)
            else:
                for ch in range(NCH):
                    arrived(m, d, s, ch)
        store(m, 0, s - 1, unpacked(rb.at[m, 0, s - 1]))
        if s < 8:
            store(m, 1, s, unpacked(rb.at[m, 1, s - 1]))

    def rows_of(index):
        return pl.ds(pl.multiple_of(index * 24, 8), 24)

    def lanes_of(g):
        return pl.ds(384 * g, 384)

    def r_pair(g):
        return remote(rp.at[1 - c, :, lanes_of(g)], rsib.at[:, lanes_of(g)], g2_s.at[g], g2_r.at[g], sibling)

    def r_sibling(g):
        go(r_pair(g))

    def r_scatter(g):
        r_pair(g).wait_recv()
        rsum[:, lanes_of(g)] = rp[c, :, lanes_of(g)] + rsib[:, lanes_of(g)]
        for k in range(1, 8):
            go(r_piece(g, k))

    def r_piece(g, k):
        src = rsum.at[rows_of(lax.rem(p + k, 8)), lanes_of(g)]
        return remote(src, rrs.at[k - 1, :, lanes_of(g)], g3_s.at[g, k - 1], g3_r.at[g, k - 1], chip(k))

    def r_whole(g, k):
        mine = rg.at[c, rows_of(p), lanes_of(g)]
        return remote(mine, mine, g5_s.at[g, k - 1], g5_r.at[g, k - 1], chip(k))

    def r_gather(g):
        total = rsum[rows_of(p), lanes_of(g)]
        for k in range(1, 8):
            r_piece(g, k).wait_recv()
            total = total + rrs[k - 1, :, lanes_of(g)]
        rg[c, rows_of(p), lanes_of(g)] = total
        for k in range(1, 8):
            go(r_whole(g, k))

    def r_last(g):
        both = rg.at[c, :, lanes_of(g)]
        return remote(both, both, g6_s.at[g], g6_r.at[g], sibling)

    def r_forward(g):
        for k in range(1, 8):
            r_whole(g, k).wait_recv()
        go(r_last(g))

    def t_partial():
        for g in range(2):
            r_last(g).wait_recv()
        factor = (split(rg[0]), split(rg[1]))
        parts = []
        for part in range(2):
            rows = slice(96 * part, 96 * part + 96)
            total = dot3(factor[0], (mh[0, rows, :], ml[0, rows, :]), NT)
            parts.append(total + dot3(factor[1], (mh[1, rows, :], ml[1, rows, :]), NT))
        for side in range(2):
            rows = slice(96 * side, 96 * side + 96)
            fold(tp.at[side], parts[0][rows, :], parts[1][rows, :])
        go(t_exchange())

    def fold(dst, first, second):
        dst[0:96, 0:96] = first
        dst[0:96, 96:128] = second[:, 0:32]
        dst[96:144, 0:64] = second[0:48, 32:96]
        dst[96:144, 64:128] = second[48:96, 32:96]

    def unfold(value):
        wide[:, 0:96] = value[0:96, 0:96]
        wide[:, 128:160] = value[0:96, 96:128]
        wide[0:48, 160:224] = value[96:144, 0:64]
        wide[48:96, 160:224] = value[96:144, 64:128]
        return wide[...]

    def t_exchange():
        return remote(tp.at[1 - h], trecv, te_s.at[0], te_r.at[0], partner)

    def t_piece(k, other):
        return remote(tfin, tg.at[c, place, h], tm_s.at[k, other], tm_r.at[k, other], near(k, other))

    def t_spread():
        t_exchange().wait_recv()
        total = tp[h] + trecv[...]
        tfin[...] = total
        tg[c, place, h] = total
        for k in range(4):
            for other in range(2):
                if k or other:
                    go(t_piece(k, other))

    def t_last():
        return remote(tg.at[c], tg.at[c], tf_s.at[0], tf_r.at[0], sibling)

    def t_forward():
        for k in range(4):
            for other in range(2):
                if k or other:
                    t_piece(k, other).wait_recv()
        go(t_last())

    def u_exchange():
        return remote(up, urecv, ue_s.at[0], ue_r.at[0], chip(4))

    def u_partial():
        t_last().wait_recv()
        for core in range(2):
            for j in range(4):
                for plane in range(2):
                    high, low = split(unfold(tg[core, j, plane]))
                    lanes = slice(256 * (2 * j + core), 256 * (2 * j + core) + 256)
                    th[96 * plane:96 * plane + 96, lanes] = high
                    tl[96 * plane:96 * plane + 96, lanes] = low
        total = dot3((th[...], tl[...]), (bh[...], bl[...]), NT)
        up[0:192, :] = total[:, 0:128]
        up[192:288, 0:64] = total[0:96, 128:192]
        up[192:288, 64:128] = total[96:192, 128:192]
        go(u_exchange())

    def v_sibling(k):
        target = lax.rem(place + k, 4)
        return remote(vp.at[1 - c, target], vsib.at[target], vs_s.at[k], vs_r.at[k], sibling)

    def v_partial():
        u_exchange().wait_recv()
        total = up[...] + urecv[...]
        turned[:, 0:128] = total[0:192, :]
        turned[0:96, 128:192] = total[192:288, 0:64]
        turned[96:192, 128:192] = total[192:288, 64:128]
        whole = split(turned[...])
        for k in range(4):
            target = lax.rem(place + k, 4)
            for core in range(2):
                lanes = pl.ds(pl.multiple_of(256 * (2 * target + core), 256), 256)
                term = dot3(whole, (ah[:, lanes], al[:, lanes]), NN)
                for side in range(2):
                    rows = slice(96 * side, 96 * side + 96)
                    fold(vp.at[core, target, side], term[rows, 0:96], term[rows, 128:224])
            go(v_sibling(k))

    def v_piece(k, other):
        src = vsum.at[lax.rem(place + k, 4), (1 - h) if other else h]
        return remote(src, vrecv.at[k, other], vr_s.at[k, other], vr_r.at[k, other], near(k, other))

    def v_scatter():
        for k in range(4):
            v_sibling(k).wait_recv()
            target = lax.rem(place + k, 4)
            vsum[target] = vp[c, target] + vsib[target]
            for other in range(2):
                if k or other:
                    go(v_piece(k, other))

    def v_result():
        total = vsum[place, h]
        for k in range(4):
            for other in range(2):
                if k or other:
                    v_piece(k, other).wait_recv()
                    total = total + vrecv[k, other]
        out = unfold(total).T
        o_ref[0:96, :] = out[0:96, :]
        o_ref[96:192, :] = out[128:224, :]

    def spread_d():
        loads[1].wait()
        dsend[:, 0:96] = inp[1]
        dsend[:, 96:128] = jnp.zeros((192, 32), F32)
        go(d_copy)

    def turn_d():
        d_copy.wait_recv()
        for ref, plane in ((dsend, h), (drecv, 1 - h)):
            high, low = split(ref[...].T[0:96, :])
            dth[pl.ds(pl.multiple_of(plane * 96, 16), 96), :] = high
            dtl[pl.ds(pl.multiple_of(plane * 96, 16), 96), :] = low
        own_block(OLD_R)

    def load_m():
        loads[2].wait()
        pack(inp.at[2], pk.at[MOM])

    locals_of = dict(
        spread_d=spread_d, turn_d=turn_d, load_m=load_m, swap_start=swap_start, swap_end=swap_end,
        r_sibling=r_sibling, r_scatter=r_scatter, r_gather=r_gather, r_forward=r_forward,
        t_partial=t_partial, t_spread=t_spread, t_forward=t_forward, u_partial=u_partial,
        v_partial=v_partial, v_scatter=v_scatter, v_result=v_result,
    )
    d_copy = remote(dsend, drecv, d_s.at[0], d_r.at[0], partner)
    tmp[:, 96:128] = jnp.zeros((192, 32), F32)
    wide[...] = jnp.zeros((96, 256), F32)
    for _, name, m, s in sorted(EVENTS):
        if name == "ring":
            if s <= 8:
                send_step(m, s)
            if s == 1 and m != OLD_R:
                own_block(m)
            if s >= 2:
                take(m, s - 1)
        elif name == "fast":
            if s < 4:
                fast_step(s)
            if s >= 1:
                take(m, 2 * s - 1)
                take(m, 2 * s)
        else:
            action = locals_of[name]
            action(m) if m is not None else action()

    for copy in finish:
        copy.wait_send()

    @pl.when(half != h)
    def _():
        for m in (OLD_L, NEW_L):
            swap(m).wait_send()


def local(basis_new_left, basis_old_left, basis_new_right, basis_old_right, moment):
    vmem, dma = pltpu.VMEM, pltpu.SemaphoreType.DMA
    scratch = [
        vmem((5, 192, 96), F32), vmem((2, 144, 128), F32), vmem((96, 256), F32), vmem((192, 192), F32),
        vmem((4, 144, 128), F32), vmem((4, 2, 8, 144, 128), F32),
        vmem((192, 128), F32), vmem((192, 128), F32), vmem((192, 192), BF16), vmem((192, 192), BF16),
        vmem((192, 128), F32),
        vmem((2, 192, 768), F32), vmem((192, 768), F32), vmem((192, 768), F32),
        vmem((7, 24, 768), F32), vmem((2, 192, 768), F32),
        vmem((2, 192, 768), BF16), vmem((2, 192, 768), BF16),
        vmem((192, 2048), BF16), vmem((192, 2048), BF16), vmem((192, 2048), BF16), vmem((192, 2048), BF16),
        vmem((2, 144, 128), F32), vmem((144, 128), F32), vmem((144, 128), F32), vmem((2, 4, 2, 144, 128), F32),
        vmem((192, 2048), BF16), vmem((192, 2048), BF16),
        vmem((288, 128), F32), vmem((288, 128), F32),
        vmem((2, 4, 2, 144, 128), F32), vmem((4, 2, 144, 128), F32), vmem((4, 2, 144, 128), F32),
        vmem((4, 2, 144, 128), F32),
        dma((5,)), dma((2,)), dma((2,)), dma((4, 2, 8, NCH)), dma((4, 2, 8, NCH)), dma((1,)), dma((1,)),
        dma((2,)), dma((2,)), dma((2, 7)), dma((2, 7)), dma((2, 7)), dma((2, 7)), dma((2,)), dma((2,)),
        dma((1,)), dma((1,)), dma((4, 2)), dma((4, 2)), dma((1,)), dma((1,)), dma((1,)), dma((1,)),
        dma((4,)), dma((4,)), dma((4, 2)), dma((4, 2)),
    ]
    return pl.pallas_call(
        kernel,
        out_shape=jax.ShapeDtypeStruct((192, 96), F32),
        in_specs=[pl.BlockSpec(memory_space=pl.ANY)] * 5,
        out_specs=pl.BlockSpec(memory_space=pltpu.VMEM),
        scratch_shapes=scratch,
        compiler_params=pltpu.CompilerParams(
            collective_id=0, has_side_effects=True, vmem_limit_bytes=56 << 20
        ),
    )(basis_old_right, moment, basis_old_left, basis_new_left, basis_new_right)


def solution(mesh):
    placed = (P("row", "col"),) * 5
    return jax.shard_map(local, mesh=mesh, in_specs=placed, out_specs=P("row", "col"), check_vma=False)
```

```python
import functools

import jax
import jax.numpy as jnp
from jax import lax
from jax.experimental import pallas as pl
from jax.experimental.pallas import tpu as pltpu
from jax.sharding import PartitionSpec as P

MESH = pl.DeviceIdType.MESH
F32, BF16 = jnp.float32, jnp.bfloat16
OLD_R, MOM, OLD_L, NEW_L = 0, 1, 2, 3
NCH = 2
FAST = (
    ((2, 1), (0,), ()), ((4, 3), (2, 1), ()), ((5,), (4, 3), (1, 2)), ((6,), (5,), (3, 4)),
    ((7,), (6,), (5,)), ((8,), (7,), (6,)), ((), (8,), (7, 8)),
)
ORDER = (
    "C0", "spread_d", "load_m", "M1", "swap_start:2", "swap_start:3", "turn_d",
    "C1", "M2", "C2", "M3", "swap_end:2", "swap_end:3",
    "C3", "r_scatter:0", "M4", "C4", "M5", "B1", "C5", "r_gather:0", "M6", "A1",
    "C6", "r_scatter:1", "M7", "B2", "A2",
    "r_gather:1", "t_first", "M8", "B3", "M9", "A3",
    "t_partial", "B4", "A4", "B5", "A5",
    "t_spread", "settle:70", "B6", "A6", "B7", "A7", "B8", "A8", "B9",
    "u_partial", "settle:20", "A9",
    "v_partial", "v_result",
)


def parsed(order):
    for token in order:
        name, _, value = token.partition(":")
        if name[0] in "CMBA":
            m = "CMBA".index(name[0])
            yield ("ring" if m else "fast"), m, int(name[1:])
        else:
            yield name, (int(value) if value else None), 0


NN = (((1,), (0,)), ((), ()))
NT = (((1,), (1,)), ((), ()))


def split(value):
    high = value.astype(BF16)
    return high, (value - high.astype(F32)).astype(BF16)


def dot3(a, b, dims):
    def one(u, v):
        return lax.dot_general(u, v, dims, preferred_element_type=F32)

    return one(a[0], b[0]) + (one(a[0], b[1]) + one(a[1], b[0]))


def kernel(c_ref, m_ref, b_ref, a_ref, d_ref, o_ref, *scratch):
    (inp, sw, wide, pk, pk2, rb, rb2, dd, dth, dtl, tmp, rp, rrs, rg, mh, ml, bh, bl, ah, al,
     tp, trecv, tfin, tg, th, tl, tsum, up, urecv, vp, vrecv,
     in_s, sw_s, sw_r, ring_s, ring_r, sh_s, sh_r, d_s, d_r, g3_s, g3_r, g5_s, g5_r,
     te_s, te_r, tm_s, tm_r, ue_s, ue_r, vr_s, vr_r) = scratch
    r, q = lax.axis_index("row"), lax.axis_index("col")
    p, c = r // 2, lax.rem(r, 2)
    h, z = q // 16, lax.rem(q, 16)
    half, place = p // 4, lax.rem(p, 4)
    sibling = (p * 2 + (1 - c), q)
    partner = (r, (1 - h) * 16 + z)
    ring_to = tuple((r, h * 16 + lax.rem(z + k, 16)) for k in (1, 15, 2, 14))

    def chip(k):
        return (lax.rem(p + k, 8) * 2 + c, q)

    def near(k, other, core=c):
        return ((4 * half + lax.rem(place + k, 4)) * 2 + core, ((1 - h) if other else h) * 16 + z)

    across = ((4 * (1 - half) + place) * 2 + c, (1 - h) * 16 + z)

    barrier = pltpu.get_barrier_semaphore()
    greeted = [sibling, across, *ring_to]
    greeted += [chip(k) for k in range(1, 8)] + [near(k, True) for k in range(4)]
    greeted += [near(k, other, 1 - c) for k in range(4) for other in range(2) if k or other]
    for device in greeted:
        pl.semaphore_signal(barrier, inc=1, device_id=device, device_id_type=MESH)

    loads = [pltpu.make_async_copy(ref, inp.at[i], in_s.at[i]) for i, ref in enumerate((c_ref, d_ref, m_ref, b_ref, a_ref))]
    for load in loads:
        load.start()

    def pack(source, dst):
        dst[:, 0:96] = source[0:144, :]
        for part in range(3):
            dst[48 * part:48 * part + 48, 96:128] = source[144:192, 32 * part:32 * part + 32]

    loads[0].wait()
    pack(inp.at[0], pk.at[OLD_R])
    tmp[:, 96:128] = jnp.zeros((192, 32), F32)
    wide[...] = jnp.zeros((96, 256), F32)
    pl.semaphore_wait(barrier, len(greeted))

    def remote(src, dst, send, recv, device):
        return pltpu.make_async_remote_copy(
            src_ref=src, dst_ref=dst, send_sem=send, recv_sem=recv, device_id=device, device_id_type=MESH
        )

    finish = []

    def settle(keep):
        while len(finish) > keep:
            finish.pop(0).wait_send()

    def go(copy):
        copy.start()
        finish.append(copy)
        return copy

    def ring(m, d, s, ch):
        if s == 8:
            rows, dst = pl.ds(72 * d, 72), rb.at[m, 0, 7]
        else:
            rows, dst = pl.ds(ch * (144 // NCH), 144 // NCH), rb.at[m, d, s - 1]
        back = 2 if m == OLD_R and s in (2, 4) else 1
        src = pk.at[m] if s == back else rb.at[m, d, s - back - 1]
        return remote(
            src.at[rows], dst.at[rows], ring_s.at[m, d, s - 1, ch], ring_r.at[m, d, s - 1, ch],
            ring_to[d + 2 * (back - 1)],
        )

    waited = set()

    def arrived(m, d, s, ch):
        if s >= 1 and (m, d, s, ch) not in waited:
            waited.add((m, d, s, ch))
            ring(m, d, s, ch).wait_recv()

    def send_step(m, s):
        for ch in range(NCH if s < 8 else 1):
            for d in range(2):
                for before in ([ch] if s < 8 else range(NCH)):
                    arrived(m, d, s - 1, before)
                go(ring(m, d, s, ch))

    def fast_step(s):
        sends, shares, takes = FAST[s]
        for offset in takes[:-1] if s == 6 else takes:
            take(OLD_R, offset)
        for ch in range(NCH):
            for offset in sends:
                if offset < 8 or ch == 0:
                    back = 2 if offset in (2, 4) else 1
                    for d in range(2):
                        if offset > back:
                            for before in ([ch] if offset < 8 else range(NCH)):
                                arrived(OLD_R, d, offset - back, before)
                        go(ring(OLD_R, d, offset, ch))
        for offset in shares:
            share(OLD_R, offset)
        if s == 6:
            take(OLD_R, takes[-1])

    def unpacked(src):
        lane = lax.broadcasted_iota(jnp.int32, (144, 128), 1)
        tmp[0:144, :] = jnp.where(lane < 96, src[...], 0.0)
        for part in range(3):
            tmp[144:192, 32 * part:32 * part + 32] = src[48 * part:48 * part + 48, 96:128]
        return split(tmp[...])

    def shared(m, d, s):
        src, dst = (pk.at[m], pk2.at[m]) if s == 0 else (rb.at[m, d, s - 1], rb2.at[m, d, s - 1])
        return remote(src, dst, sh_s.at[m, d, s], sh_r.at[m, d, s], sibling)

    def share(m, s):
        for d in range(2 if 0 < s < 8 else 1):
            if s > 0:
                for ch in range(NCH if s < 8 else 1):
                    arrived(m, d, s, ch)
            if s == 8:
                arrived(m, 1, 8, 0)
            go(shared(m, d, s))

    def store(m, d, e, own, other):
        one, two = unpacked(own), unpacked(other)
        high, low = (jnp.concatenate([u, v], axis=0) for u, v in zip(one, two))
        if m == OLD_R:
            rp[d, :, 96 * e:96 * e + 96] = dot3((dth[...], dtl[...]), (high, low), NN)[:, 0:96]
        elif m == MOM:
            mh[d, :, 96 * e:96 * e + 96] = high[:, 0:96]
            ml[d, :, 96 * e:96 * e + 96] = low[:, 0:96]
        else:
            origin = lax.rem(z + (16 - (e + 1) if d == 0 else e), 16)
            lanes = pl.ds(pl.multiple_of(origin * 128, 128), 128)
            hs, ls = (bh, bl) if m == OLD_L else (ah, al)
            hs[:, lanes] = high
            ls[:, lanes] = low

    def take(m, s):
        for d in range(2 if 0 < s < 8 else 1):
            shared(m, d, s).wait_recv()
        if s == 0:
            store(m, 1, 0, pk.at[m], pk2.at[m])
        else:
            store(m, 0, s - 1, rb.at[m, 0, s - 1], rb2.at[m, 0, s - 1])
            if s < 8:
                store(m, 1, s, rb.at[m, 1, s - 1], rb2.at[m, 1, s - 1])

    def swap(m):
        return remote(sw.at[m - 2], pk.at[m], sw_s.at[m - 2], sw_r.at[m - 2], across)

    def swap_start(m):
        loads[m + 1].wait()
        pack(inp.at[m + 1], sw.at[m - 2])

        @pl.when(half != h)
        def _():
            swap(m).start()

        @pl.when(half == h)
        def _():
            pltpu.make_async_copy(sw.at[m - 2], pk.at[m], sw_r.at[m - 2]).start()

    def swap_end(m):
        pltpu.make_async_copy(sw.at[m - 2], pk.at[m], sw_r.at[m - 2]).wait()
        share(m, 0)

    def r_piece(g, k):
        target = lax.rem(p + k, 8)
        rows = pl.ds(pl.multiple_of(target // 2 * 24, 8), 24)
        lanes = pl.ds(384 * g, 384)
        return remote(
            rp.at[lax.rem(target, 2), rows, lanes], rrs.at[k - 1, :, lanes], g3_s.at[g, k - 1], g3_r.at[g, k - 1], chip(k)
        )

    my_rows = pl.ds(pl.multiple_of(p // 2 * 24, 8), 24)

    def r_whole(g, k):
        mine = rg.at[lax.rem(p, 2), my_rows, pl.ds(384 * g, 384)]
        return remote(mine, mine, g5_s.at[g, k - 1], g5_r.at[g, k - 1], chip(k))

    def r_scatter(g):
        for k in range(1, 8):
            go(r_piece(g, k))

    def r_gather(g):
        lanes = pl.ds(384 * g, 384)
        total = rp[lax.rem(p, 2), my_rows, lanes]
        for k in range(1, 8):
            r_piece(g, k).wait_recv()
            total = total + rrs[k - 1, :, lanes]
        rg[lax.rem(p, 2), my_rows, lanes] = total
        for k in range(1, 8):
            go(r_whole(g, k))

    def t_half(g):
        for k in range(1, 8):
            r_whole(g, k).wait_recv()
        lanes = slice(384 * g, 384 * g + 384)
        total = None
        for d in range(2):
            term = dot3(split(rg[d, :, lanes]), (mh[d, :, lanes], ml[d, :, lanes]), NT)
            total = term if total is None else total + term
        return total

    def t_first():
        tsum[...] = t_half(0)

    def t_partial():
        total = tsum[...] + t_half(1)
        fold(tp.at[c], total[:, 0:96], total[:, 96:192])
        fold(tp.at[1 - c], total[:, 192:288], total[:, 288:384])
        go(t_exchange())

    def fold(dst, first, second):
        dst[0:96, 0:96] = first
        dst[0:96, 96:128] = second[:, 0:32]
        dst[96:144, 0:64] = second[0:48, 32:96]
        dst[96:144, 64:128] = second[48:96, 32:96]

    def unfold(value):
        wide[:, 0:96] = value[0:96, 0:96]
        wide[:, 128:160] = value[0:96, 96:128]
        wide[0:48, 160:224] = value[96:144, 0:64]
        wide[48:96, 160:224] = value[96:144, 64:128]
        return wide[...]

    def t_exchange():
        return remote(tp.at[1 - h], trecv, te_s.at[0], te_r.at[0], partner)

    def t_piece(k, other):
        return remote(tfin, tg.at[place, h], tm_s.at[k, other], tm_r.at[k, other], near(k, other))

    def t_spread():
        t_exchange().wait_recv()
        total = tp[h] + trecv[...]
        tfin[...] = total
        tg[place, h] = total
        for k in range(4):
            for other in range(2):
                if k or other:
                    go(t_piece(k, other))

    def u_exchange():
        return remote(up, urecv, ue_s.at[0], ue_r.at[0], chip(4))

    def u_partial():
        total = None
        for k in (0, 1, 3, 2):
            j = lax.rem(place + k, 4)
            for other in range(2):
                if k or other:
                    t_piece((4 - k) % 4, other).wait_recv()
            for core in range(2):
                lanes = slice(256 * core, 256 * core + 256)
                th[:, lanes], tl[:, lanes] = split(unfold(tg[j, core]))
            lanes = pl.ds(pl.multiple_of(512 * j, 512), 512)
            term = dot3((th[...], tl[...]), (bh[:, lanes], bl[:, lanes]), NT)
            total = term if total is None else total + term
        up[...] = total
        go(u_exchange())

    def v_piece(k, far):
        core = (1 - c) if far else c
        target = lax.rem(place + k, 4)
        device = ((4 * half + target) * 2 + core, c * 16 + z)
        return remote(vp.at[target, core], vrecv.at[k, h], vr_s.at[k, far], vr_r.at[k, h], device)

    def v_partial():
        u_exchange().wait_recv()
        whole = split(up[...] + urecv[...])
        for k in (1, 2, 3, 0):
            target = lax.rem(place + k, 4)
            for far in range(2):
                core = (1 - c) if far else c
                lanes = pl.ds(pl.multiple_of(256 * (2 * target + core), 256), 256)
                term = dot3(whole, (ah[:, lanes], al[:, lanes]), NN)
                fold(vp.at[target, core], term[:, 0:96], term[:, 128:224])
                if k or far:
                    go(v_piece(k, far))

        @pl.when(h != c)
        def _():
            v_piece(0, 0).start()

        @pl.when(h == c)
        def _():
            pltpu.make_async_copy(vp.at[place, c], vrecv.at[0, h], vr_r.at[0, h]).start()

    def v_result():
        total = None
        for k in range(4):
            for plane in range(2):
                pltpu.make_async_copy(vp.at[0, 0], vrecv.at[k, plane], vr_r.at[k, plane]).wait()
                total = vrecv[k, plane] if total is None else total + vrecv[k, plane]
        out = unfold(total).T
        o_ref[0:96, :] = out[0:96, :]
        o_ref[96:192, :] = out[128:224, :]

    row_of = lax.rem(c + h, 2)

    def d_near():
        return remote(inp.at[1], dd.at[row_of], d_s.at[0], d_r.at[row_of], sibling)

    def d_far():
        return remote(inp.at[1], dd.at[row_of], d_s.at[1], d_r.at[row_of], (p * 2 + h, (1 - h) * 16 + z))

    def spread_d():
        loads[1].wait()
        go(d_far())

        @pl.when(c != h)
        def _():
            d_near().start()

        @pl.when(c == h)
        def _():
            pltpu.make_async_copy(inp.at[1], dd.at[0], d_r.at[0]).start()

    def turn_d():
        for i in range(2):
            pltpu.make_async_copy(inp.at[1], dd.at[i], d_r.at[i]).wait()
            tmp[:, 0:96] = dd[i]
            dth[:, 192 * i:192 * i + 192], dtl[:, 192 * i:192 * i + 192] = split(tmp[...].T[0:96, :])
        take(OLD_R, 0)

    def load_m():
        loads[2].wait()
        pack(inp.at[2], pk.at[MOM])
        share(MOM, 0)

    locals_of = dict(
        spread_d=spread_d, turn_d=turn_d, load_m=load_m, swap_start=swap_start, swap_end=swap_end,
        r_scatter=r_scatter, r_gather=r_gather, t_first=t_first, t_partial=t_partial, t_spread=t_spread, u_partial=u_partial,
        v_partial=v_partial, v_result=v_result, settle=settle,
    )
    for name, m, s in parsed(ORDER):
        if name == "ring":
            if s >= 2:
                take(m, s - 2)
            if s <= 8:
                send_step(m, s)
            if s >= 2:
                share(m, s - 1)
            if s == 9:
                take(m, 8)
        elif name == "fast":
            fast_step(s)
        else:
            action = locals_of[name]
            action(m) if m is not None else action()

    settle(0)

    @pl.when(half != h)
    def _():
        for m in (OLD_L, NEW_L):
            swap(m).wait_send()

    @pl.when(c != h)
    def _():
        d_near().wait_send()
        v_piece(0, 0).wait_send()


def local(basis_new_left, basis_old_left, basis_new_right, basis_old_right, moment):
    vmem, dma = pltpu.VMEM, pltpu.SemaphoreType.DMA
    scratch = [
        vmem((5, 192, 96), F32), vmem((2, 144, 128), F32), vmem((96, 256), F32),
        vmem((4, 144, 128), F32), vmem((4, 144, 128), F32),
        vmem((4, 2, 8, 144, 128), F32), vmem((4, 2, 8, 144, 128), F32),
        vmem((2, 192, 96), F32), vmem((96, 384), BF16), vmem((96, 384), BF16), vmem((192, 128), F32),
        vmem((2, 96, 768), F32), vmem((7, 24, 768), F32), vmem((2, 96, 768), F32),
        vmem((2, 384, 768), BF16), vmem((2, 384, 768), BF16),
        vmem((384, 2048), BF16), vmem((384, 2048), BF16), vmem((384, 2048), BF16), vmem((384, 2048), BF16),
        vmem((2, 144, 128), F32), vmem((144, 128), F32), vmem((144, 128), F32), vmem((4, 2, 144, 128), F32),
        vmem((96, 512), BF16), vmem((96, 512), BF16), vmem((96, 384), F32), vmem((96, 384), F32), vmem((96, 384), F32),
        vmem((4, 2, 144, 128), F32), vmem((4, 2, 144, 128), F32),
        dma((5,)), dma((2,)), dma((2,)), dma((4, 2, 8, NCH)), dma((4, 2, 8, NCH)), dma((4, 2, 9)), dma((4, 2, 9)),
        dma((2,)), dma((2,)), dma((2, 7)), dma((2, 7)), dma((2, 7)), dma((2, 7)),
        dma((1,)), dma((1,)), dma((4, 2)), dma((4, 2)), dma((1,)), dma((1,)), dma((4, 2)), dma((4, 2)),
    ]
    return pl.pallas_call(
        kernel,
        out_shape=jax.ShapeDtypeStruct((192, 96), F32),
        in_specs=[pl.BlockSpec(memory_space=pl.ANY)] * 5,
        out_specs=pl.BlockSpec(memory_space=pltpu.VMEM),
        scratch_shapes=scratch,
        compiler_params=pltpu.CompilerParams(
            collective_id=0, has_side_effects=True, vmem_limit_bytes=56 << 20
        ),
    )(basis_old_right, moment, basis_old_left, basis_new_left, basis_new_right)


def solution(mesh):
    placed = (P("row", "col"),) * 5
    return jax.shard_map(local, mesh=mesh, in_specs=placed, out_specs=P("row", "col"), check_vma=False)
```

```python
import functools

import jax
import jax.numpy as jnp
from jax import lax
from jax.experimental import pallas as pl
from jax.experimental.pallas import tpu as pltpu
from jax.sharding import PartitionSpec as P

MESH = pl.DeviceIdType.MESH
F32, BF16 = jnp.float32, jnp.bfloat16
OLD_R, MOM, OLD_L, NEW_L = 0, 1, 2, 3
NCH = 2
FAST = (
    ((2, 1), (0,), ()), ((4, 3), (2, 1), ()), ((5,), (4, 3), (1, 2)), ((6,), (5,), (3, 4)),
    ((7,), (6,), (5,)), ((8,), (7,), (6,)), ((), (8,), (7, 8)),
)
ORDER = (
    "C0", "spread_d", "load_m", "M1", "swap_start:2", "swap_start:3", "turn_d",
    "C1", "M2", "C2", "M3", "swap_end:2", "swap_end:3",
    "C3", "r_scatter:0", "M4", "C4", "M5", "B1", "C5", "r_gather:0", "M6", "A1",
    "C6", "r_scatter:1", "M7", "B2", "A2",
    "r_gather:1", "t_first", "M8", "B3", "M9", "A3",
    "t_partial", "B4", "A4", "B5", "A5",
    "t_spread", "settle:70", "B6", "A6", "B7", "A7", "B8", "A8", "B9",
    "u_partial", "settle:20", "A9",
    "v_partial", "v_result",
)


def parsed(order):
    for token in order:
        name, _, value = token.partition(":")
        if name[0] in "CMBA":
            m = "CMBA".index(name[0])
            yield ("ring" if m else "fast"), m, int(name[1:])
        else:
            yield name, (int(value) if value else None), 0


NN = (((1,), (0,)), ((), ()))
NT = (((1,), (1,)), ((), ()))


def split(value):
    high = value.astype(BF16)
    return high, (value - high.astype(F32)).astype(BF16)


def dot3(a, b, dims):
    def one(u, v):
        return lax.dot_general(u, v, dims, preferred_element_type=F32)

    return one(a[0], b[0]) + (one(a[0], b[1]) + one(a[1], b[0]))


def kernel(c_ref, m_ref, b_ref, a_ref, d_ref, o_ref, *scratch):
    (inp, sw, wide, pk, pk2, rb, rb2, dd, dth, dtl, tmp, rp, rrs, rg, mh, ml, bh, bl, ah, al,
     tp, trecv, tfin, tg, th, tl, tsum, up, urecv, vp, vrecv,
     in_s, sw_s, sw_r, ring_s, ring_r, sh_s, sh_r, d_s, d_r, g3_s, g3_r, g5_s, g5_r,
     te_s, te_r, tm_s, tm_r, ue_s, ue_r, vr_s, vr_r) = scratch
    r, q = lax.axis_index("row"), lax.axis_index("col")
    p, c = r // 2, lax.rem(r, 2)
    h, z = q // 16, lax.rem(q, 16)
    half, place = p // 4, lax.rem(p, 4)
    sibling = (p * 2 + (1 - c), q)
    partner = (r, (1 - h) * 16 + z)
    ring_to = tuple((r, h * 16 + lax.rem(z + k, 16)) for k in (1, 15, 2, 14))

    def chip(k):
        return (lax.rem(p + k, 8) * 2 + c, q)

    def near(k, other, core=c):
        return ((4 * half + lax.rem(place + k, 4)) * 2 + core, ((1 - h) if other else h) * 16 + z)

    across = ((4 * (1 - half) + place) * 2 + c, (1 - h) * 16 + z)

    loads = [pltpu.make_async_copy(ref, inp.at[i], in_s.at[i]) for i, ref in enumerate((c_ref, d_ref, m_ref, b_ref, a_ref))]
    for load in loads:
        load.start()

    barrier = pltpu.get_barrier_semaphore()
    greeted = [across]
    greeted += [near(k, other, 1 - c) for k in range(4) for other in range(2) if k or other]
    greeted += [near(k, True) for k in range(4)] + [chip(k) for k in range(1, 8)] + [*ring_to, sibling]
    for device in greeted:
        pl.semaphore_signal(barrier, inc=1, device_id=device, device_id_type=MESH)

    def pack(source, dst):
        dst[:, 0:96] = source[0:144, :]
        for part in range(3):
            dst[48 * part:48 * part + 48, 96:128] = source[144:192, 32 * part:32 * part + 32]

    loads[0].wait()
    pack(inp.at[0], pk.at[OLD_R])
    tmp[:, 96:128] = jnp.zeros((192, 32), F32)
    wide[...] = jnp.zeros((96, 256), F32)
    pl.semaphore_wait(barrier, len(greeted))

    def remote(src, dst, send, recv, device):
        return pltpu.make_async_remote_copy(
            src_ref=src, dst_ref=dst, send_sem=send, recv_sem=recv, device_id=device, device_id_type=MESH
        )

    finish = []

    def settle(keep):
        while len(finish) > keep:
            finish.pop(0).wait_send()

    def go(copy):
        copy.start()
        finish.append(copy)
        return copy

    def ring(m, d, s, ch):
        if s == 8:
            rows, dst = pl.ds(72 * d, 72), rb.at[m, 0, 7]
        else:
            rows, dst = pl.ds(ch * (144 // NCH), 144 // NCH), rb.at[m, d, s - 1]
        back = 2 if m == OLD_R and s in (2, 4) else 1
        src = pk.at[m] if s == back else rb.at[m, d, s - back - 1]
        return remote(
            src.at[rows], dst.at[rows], ring_s.at[m, d, s - 1, ch], ring_r.at[m, d, s - 1, ch],
            ring_to[d + 2 * (back - 1)],
        )

    waited = set()

    def arrived(m, d, s, ch):
        if s >= 1 and (m, d, s, ch) not in waited:
            waited.add((m, d, s, ch))
            ring(m, d, s, ch).wait_recv()

    def send_step(m, s):
        for ch in range(NCH if s < 8 else 1):
            for d in range(2):
                for before in ([ch] if s < 8 else range(NCH)):
                    arrived(m, d, s - 1, before)
                go(ring(m, d, s, ch))

    def fast_step(s):
        sends, shares, takes = FAST[s]
        for offset in takes[:-1] if s == 6 else takes:
            take(OLD_R, offset)
        for ch in range(NCH):
            for offset in sends:
                if offset < 8 or ch == 0:
                    back = 2 if offset in (2, 4) else 1
                    for d in range(2):
                        if offset > back:
                            for before in ([ch] if offset < 8 else range(NCH)):
                                arrived(OLD_R, d, offset - back, before)
                        go(ring(OLD_R, d, offset, ch))
        for offset in shares:
            share(OLD_R, offset)
        if s == 6:
            take(OLD_R, takes[-1])

    def unpacked(src):
        lane = lax.broadcasted_iota(jnp.int32, (144, 128), 1)
        tmp[0:144, :] = jnp.where(lane < 96, src[...], 0.0)
        for part in range(3):
            tmp[144:192, 32 * part:32 * part + 32] = src[48 * part:48 * part + 48, 96:128]
        return split(tmp[...])

    def shared(m, d, s):
        src, dst = (pk.at[m], pk2.at[m]) if s == 0 else (rb.at[m, d, s - 1], rb2.at[m, d, s - 1])
        return remote(src, dst, sh_s.at[m, d, s], sh_r.at[m, d, s], sibling)

    def share(m, s):
        for d in range(2 if 0 < s < 8 else 1):
            if s > 0:
                for ch in range(NCH if s < 8 else 1):
                    arrived(m, d, s, ch)
            if s == 8:
                arrived(m, 1, 8, 0)
            go(shared(m, d, s))

    def store(m, d, e, own, other):
        one, two = unpacked(own), unpacked(other)
        high, low = (jnp.concatenate([u, v], axis=0) for u, v in zip(one, two))
        if m == OLD_R:
            rp[d, :, 96 * e:96 * e + 96] = dot3((dth[...], dtl[...]), (high, low), NN)[:, 0:96]
        elif m == MOM:
            mh[d, :, 96 * e:96 * e + 96] = high[:, 0:96]
            ml[d, :, 96 * e:96 * e + 96] = low[:, 0:96]
        else:
            origin = lax.rem(z + (16 - (e + 1) if d == 0 else e), 16)
            lanes = pl.ds(pl.multiple_of(origin * 128, 128), 128)
            hs, ls = (bh, bl) if m == OLD_L else (ah, al)
            hs[:, lanes] = high
            ls[:, lanes] = low

    def take(m, s):
        for d in range(2 if 0 < s < 8 else 1):
            shared(m, d, s).wait_recv()
        if s == 0:
            store(m, 1, 0, pk.at[m], pk2.at[m])
        else:
            store(m, 0, s - 1, rb.at[m, 0, s - 1], rb2.at[m, 0, s - 1])
            if s < 8:
                store(m, 1, s, rb.at[m, 1, s - 1], rb2.at[m, 1, s - 1])

    def swap(m):
        return remote(sw.at[m - 2], pk.at[m], sw_s.at[m - 2], sw_r.at[m - 2], across)

    def swap_start(m):
        loads[m + 1].wait()
        pack(inp.at[m + 1], sw.at[m - 2])

        @pl.when(half != h)
        def _():
            swap(m).start()

        @pl.when(half == h)
        def _():
            pltpu.make_async_copy(sw.at[m - 2], pk.at[m], sw_r.at[m - 2]).start()

    def swap_end(m):
        pltpu.make_async_copy(sw.at[m - 2], pk.at[m], sw_r.at[m - 2]).wait()
        share(m, 0)

    def r_piece(g, k):
        target = lax.rem(p + k, 8)
        rows = pl.ds(pl.multiple_of(target // 2 * 24, 8), 24)
        lanes = pl.ds(384 * g, 384)
        return remote(
            rp.at[lax.rem(target, 2), rows, lanes], rrs.at[k - 1, :, lanes], g3_s.at[g, k - 1], g3_r.at[g, k - 1], chip(k)
        )

    my_rows = pl.ds(pl.multiple_of(p // 2 * 24, 8), 24)

    def r_whole(g, k):
        mine = rg.at[lax.rem(p, 2), my_rows, pl.ds(384 * g, 384)]
        return remote(mine, mine, g5_s.at[g, k - 1], g5_r.at[g, k - 1], chip(k))

    def r_scatter(g):
        for k in range(1, 8):
            go(r_piece(g, k))

    def r_gather(g):
        lanes = pl.ds(384 * g, 384)
        total = rp[lax.rem(p, 2), my_rows, lanes]
        for k in range(1, 8):
            r_piece(g, k).wait_recv()
            total = total + rrs[k - 1, :, lanes]
        rg[lax.rem(p, 2), my_rows, lanes] = total
        for k in range(1, 8):
            go(r_whole(g, k))

    def t_half(g):
        for k in range(1, 8):
            r_whole(g, k).wait_recv()
        lanes = slice(384 * g, 384 * g + 384)
        total = None
        for d in range(2):
            term = dot3(split(rg[d, :, lanes]), (mh[d, :, lanes], ml[d, :, lanes]), NT)
            total = term if total is None else total + term
        return total

    def t_first():
        tsum[...] = t_half(0)

    def t_partial():
        total = tsum[...] + t_half(1)
        fold(tp.at[c], total[:, 0:96], total[:, 96:192])
        fold(tp.at[1 - c], total[:, 192:288], total[:, 288:384])
        go(t_exchange())

    def fold(dst, first, second):
        dst[0:96, 0:96] = first
        dst[0:96, 96:128] = second[:, 0:32]
        dst[96:144, 0:64] = second[0:48, 32:96]
        dst[96:144, 64:128] = second[48:96, 32:96]

    def unfold(value):
        wide[:, 0:96] = value[0:96, 0:96]
        wide[:, 128:160] = value[0:96, 96:128]
        wide[0:48, 160:224] = value[96:144, 0:64]
        wide[48:96, 160:224] = value[96:144, 64:128]
        return wide[...]

    def t_exchange():
        return remote(tp.at[1 - h], trecv, te_s.at[0], te_r.at[0], partner)

    def t_piece(k, other):
        return remote(tfin, tg.at[place, h], tm_s.at[k, other], tm_r.at[k, other], near(k, other))

    def t_spread():
        t_exchange().wait_recv()
        total = tp[h] + trecv[...]
        tfin[...] = total
        tg[place, h] = total
        for k in range(4):
            for other in range(2):
                if k or other:
                    go(t_piece(k, other))

    def u_exchange():
        return remote(up, urecv, ue_s.at[0], ue_r.at[0], chip(4))

    def u_partial():
        total = None
        for k in (0, 1, 3, 2):
            j = lax.rem(place + k, 4)
            for other in range(2):
                if k or other:
                    t_piece((4 - k) % 4, other).wait_recv()
            for core in range(2):
                lanes = slice(256 * core, 256 * core + 256)
                th[:, lanes], tl[:, lanes] = split(unfold(tg[j, core]))
            lanes = pl.ds(pl.multiple_of(512 * j, 512), 512)
            term = dot3((th[...], tl[...]), (bh[:, lanes], bl[:, lanes]), NT)
            total = term if total is None else total + term
        up[...] = total
        go(u_exchange())

    def v_piece(k, far):
        core = (1 - c) if far else c
        target = lax.rem(place + k, 4)
        device = ((4 * half + target) * 2 + core, c * 16 + z)
        return remote(vp.at[target, core], vrecv.at[k, h], vr_s.at[k, far], vr_r.at[k, h], device)

    def v_partial():
        u_exchange().wait_recv()
        whole = split(up[...] + urecv[...])
        for k in (1, 2, 3, 0):
            target = lax.rem(place + k, 4)
            for far in range(2):
                core = (1 - c) if far else c
                lanes = pl.ds(pl.multiple_of(256 * (2 * target + core), 256), 256)
                term = dot3(whole, (ah[:, lanes], al[:, lanes]), NN)
                fold(vp.at[target, core], term[:, 0:96], term[:, 128:224])
                if k or far:
                    go(v_piece(k, far))

        @pl.when(h != c)
        def _():
            v_piece(0, 0).start()

        @pl.when(h == c)
        def _():
            pltpu.make_async_copy(vp.at[place, c], vrecv.at[0, h], vr_r.at[0, h]).start()

    def v_result():
        total = None
        for k in range(4):
            for plane in range(2):
                pltpu.make_async_copy(vp.at[0, 0], vrecv.at[k, plane], vr_r.at[k, plane]).wait()
                total = vrecv[k, plane] if total is None else total + vrecv[k, plane]
        out = unfold(total).T
        o_ref[0:96, :] = out[0:96, :]
        o_ref[96:192, :] = out[128:224, :]

    row_of = lax.rem(c + h, 2)

    def d_near():
        return remote(inp.at[1], dd.at[row_of], d_s.at[0], d_r.at[row_of], sibling)

    def d_far():
        return remote(inp.at[1], dd.at[row_of], d_s.at[1], d_r.at[row_of], (p * 2 + h, (1 - h) * 16 + z))

    def spread_d():
        loads[1].wait()
        go(d_far())

        @pl.when(c != h)
        def _():
            d_near().start()

        @pl.when(c == h)
        def _():
            pltpu.make_async_copy(inp.at[1], dd.at[0], d_r.at[0]).start()

    def turn_d():
        for i in range(2):
            pltpu.make_async_copy(inp.at[1], dd.at[i], d_r.at[i]).wait()
            tmp[:, 0:96] = dd[i]
            dth[:, 192 * i:192 * i + 192], dtl[:, 192 * i:192 * i + 192] = split(tmp[...].T[0:96, :])
        take(OLD_R, 0)

    def load_m():
        loads[2].wait()
        pack(inp.at[2], pk.at[MOM])
        share(MOM, 0)

    locals_of = dict(
        spread_d=spread_d, turn_d=turn_d, load_m=load_m, swap_start=swap_start, swap_end=swap_end,
        r_scatter=r_scatter, r_gather=r_gather, t_first=t_first, t_partial=t_partial, t_spread=t_spread, u_partial=u_partial,
        v_partial=v_partial, v_result=v_result, settle=settle,
    )
    for name, m, s in parsed(ORDER):
        if name == "ring":
            if s >= 2:
                take(m, s - 2)
            if s <= 8:
                send_step(m, s)
            if s >= 2:
                share(m, s - 1)
            if s == 9:
                take(m, 8)
        elif name == "fast":
            fast_step(s)
        else:
            action = locals_of[name]
            action(m) if m is not None else action()

    settle(0)

    @pl.when(half != h)
    def _():
        for m in (OLD_L, NEW_L):
            swap(m).wait_send()

    @pl.when(c != h)
    def _():
        d_near().wait_send()
        v_piece(0, 0).wait_send()


def local(basis_new_left, basis_old_left, basis_new_right, basis_old_right, moment):
    vmem, dma = pltpu.VMEM, pltpu.SemaphoreType.DMA
    scratch = [
        vmem((5, 192, 96), F32), vmem((2, 144, 128), F32), vmem((96, 256), F32),
        vmem((4, 144, 128), F32), vmem((4, 144, 128), F32),
        vmem((4, 2, 8, 144, 128), F32), vmem((4, 2, 8, 144, 128), F32),
        vmem((2, 192, 96), F32), vmem((96, 384), BF16), vmem((96, 384), BF16), vmem((192, 128), F32),
        vmem((2, 96, 768), F32), vmem((7, 24, 768), F32), vmem((2, 96, 768), F32),
        vmem((2, 384, 768), BF16), vmem((2, 384, 768), BF16),
        vmem((384, 2048), BF16), vmem((384, 2048), BF16), vmem((384, 2048), BF16), vmem((384, 2048), BF16),
        vmem((2, 144, 128), F32), vmem((144, 128), F32), vmem((144, 128), F32), vmem((4, 2, 144, 128), F32),
        vmem((96, 512), BF16), vmem((96, 512), BF16), vmem((96, 384), F32), vmem((96, 384), F32), vmem((96, 384), F32),
        vmem((4, 2, 144, 128), F32), vmem((4, 2, 144, 128), F32),
        dma((5,)), dma((2,)), dma((2,)), dma((4, 2, 8, NCH)), dma((4, 2, 8, NCH)), dma((4, 2, 9)), dma((4, 2, 9)),
        dma((2,)), dma((2,)), dma((2, 7)), dma((2, 7)), dma((2, 7)), dma((2, 7)),
        dma((1,)), dma((1,)), dma((4, 2)), dma((4, 2)), dma((1,)), dma((1,)), dma((4, 2)), dma((4, 2)),
    ]
    return pl.pallas_call(
        kernel,
        out_shape=jax.ShapeDtypeStruct((192, 96), F32),
        in_specs=[pl.BlockSpec(memory_space=pl.ANY)] * 5,
        out_specs=pl.BlockSpec(memory_space=pltpu.VMEM),
        scratch_shapes=scratch,
        compiler_params=pltpu.CompilerParams(
            collective_id=0, has_side_effects=True, vmem_limit_bytes=56 << 20
        ),
    )(basis_old_right, moment, basis_old_left, basis_new_left, basis_new_right)


def solution(mesh):
    placed = (P("row", "col"),) * 5
    return jax.shard_map(local, mesh=mesh, in_specs=placed, out_specs=P("row", "col"), check_vma=False)
```
